32 devices in a mesh: dp: 8 (over y, x, core), index: 4 (over z).
Axes of the slice: x: 2, y: 2, z: 4, core: 2. Of those that a mesh axis runs over, the one named last changes fastest.
Arguments:
- queries: bfloat16 [4096, 1024], P(('dp', 'index')), may hold values from -0.1875 to 0.1875
- keys: bfloat16 [2048, 1024], P(('dp', 'index')), may hold values from -6 to 6
- pattern: int32 [32, 256], P(('dp', 'index')), may hold values 0 or 1
- clusters: int32 [2048], P(('dp', 'index')), may hold values from 0 to 255
- positives: int32 [4096], P(('dp', 'index')), may hold values from 0 to 2047
- loss_multiplier: float32 [4096], P(('dp', 'index')), may hold values from -4 to 4
Outputs:
- query_grad: float32 [4096, 1024], P(('dp', 'index'))
- loss: float32 [4096], P(('dp', 'index'))
The draws below stay inside these ranges and needn't reach their ends.
All inputs are finite; a program needn't handle non-finite values. No bound on the sum of `pattern` on one device may be relied on, other than what follows from the above.
Results may differ from the reference program's by a relative error of at most 0.0029.
Values may be sent and summed in bfloat16 or wider, within the bound.
No kernel may reach another device: no remote copies, remote signals or barrier semaphores. Data moves between devices by JAX's collectives and lax.ppermute only.
A program may use at most 64 MiB of HBM per device.

```python
import math
import jax
import jax.numpy as jnp
from jax import lax

D = 1024
QBLK = 128
NCB = 256
NQ = 4096
NQB = 32
NKEYS = 2048


def with_ends(array, key, least, high):
    longest = array.shape.index(max(array.shape))
    spots = []
    for shift in (0, 1):
        where = [jax.random.randint(jax.random.fold_in(key, axis), (), 0, length) for axis, length in enumerate(array.shape)]
        where[longest] = (where[longest] + shift) % array.shape[longest]
        spots.append(tuple(where))
    return array.at[spots[0]].set(least).at[spots[1]].set(high)


def block_levels(stream_key, extent, cuts, smallest, top_value):
    factor_of = 1.0
    for axis_at, shards_of in cuts:
        heights = jax.random.uniform(jax.random.fold_in(jax.random.fold_in(stream_key, 6), axis_at), (shards_of,), jnp.float32, smallest / len(cuts), top_value / len(cuts))
        factor_of = factor_of * jnp.repeat(jnp.exp(heights), extent[axis_at] // shards_of).reshape((-1,) + (1,) * (len(extent) - 1 - axis_at))
    return factor_of


def normal_values(stream_key, extent, width, reach, cuts=(), kind=jnp.bfloat16):
    gain = block_levels(stream_key, extent, cuts, -0.22, 0.18) if cuts else 1.0
    result = jax.random.normal(stream_key, extent, jnp.float32) * width * gain
    return jnp.minimum(jnp.maximum(result, -reach), reach).astype(kind)


def setup_inputs(seed: int = 0) -> dict:
    arg_keys = jax.random.split(jax.random.key(seed), 7)
    queries = normal_values(arg_keys[0], (NQ, D), 0.03125, 0.1875, ((0, 32),))
    keys = normal_values(arg_keys[1], (NKEYS, D), 1.0, 6.0, ((0, 32),))
    pattern = with_ends((jax.random.randint(arg_keys[2], (NQB, NCB), 0, 2) < 1).astype(jnp.int32), jax.random.fold_in(arg_keys[2], 1), 0, 1)
    clusters = with_ends(jax.random.randint(arg_keys[3], (NKEYS,), 0, NCB), jax.random.fold_in(arg_keys[3], 1), 0, NCB - 1).astype(jnp.int32)
    positives = with_ends(jax.random.randint(arg_keys[4], (NQ,), 0, NKEYS), jax.random.fold_in(arg_keys[4], 1), 0, NKEYS - 1).astype(jnp.int32)
    loss_multiplier = normal_values(arg_keys[5], (NQ,), 1.0, 4.0, ((0, 32),), jnp.float32)
    return dict(queries=queries, keys=keys, pattern=pattern, clusters=clusters, positives=positives, loss_multiplier=loss_multiplier)


logit_divisor = 0.1
epsilon = 1e-06

def reference(queries, keys, pattern, clusters, positives, loss_multiplier):
    query_floats = queries.astype(jnp.float32)
    query_scale = lax.rsqrt(lax.optimization_barrier(jnp.sum(query_floats * query_floats, axis=1, keepdims=True)) + epsilon)
    query_norm = (query_floats * query_scale).astype(jnp.bfloat16)
    key_floats = keys.astype(jnp.float32)
    passage_magnitude = (key_floats * lax.rsqrt(lax.optimization_barrier(jnp.sum(key_floats * key_floats, axis=1, keepdims=True)) + epsilon)).astype(jnp.bfloat16)
    key_ids = jnp.arange(NKEYS, dtype=jnp.int32)
    cluster_table = (clusters[:, None] == jnp.arange(NCB, dtype=jnp.int32)[None, :]).astype(jnp.float32)
    block_rows = math.gcd(NQ, 1024)
    block_count = NQ // block_rows

    def one_block(block_index):
        first_row = (block_index * block_rows).astype(jnp.int32)
        question_batch_slab = lax.dynamic_slice_in_dim(query_norm, first_row, block_rows, 0)
        block_marks = lax.dynamic_slice_in_dim(pattern, (first_row // QBLK).astype(jnp.int32), block_rows // QBLK, 0).astype(jnp.float32)
        allowed = jnp.dot(block_marks, cluster_table.T, precision=lax.Precision.HIGHEST)
        allowed = jnp.repeat(allowed, QBLK, axis=0)
        wanted = lax.dynamic_slice_in_dim(positives, first_row, block_rows, 0)
        is_positive = (key_ids[None, :] == wanted[:, None]).astype(jnp.float32)
        inner_product_matrix = jnp.dot(question_batch_slab, passage_magnitude.T, preferred_element_type=jnp.float32) / logit_divisor
        weights = jnp.exp(inner_product_matrix) * jnp.maximum(allowed, is_positive)
        totals = lax.optimization_barrier(jnp.sum(weights, axis=1))
        positive_scores = lax.optimization_barrier(jnp.sum(inner_product_matrix * is_positive, axis=1))
        expected = jnp.dot(weights.astype(jnp.bfloat16), passage_magnitude, preferred_element_type=jnp.float32)
        positive_keys = passage_magnitude[wanted].astype(jnp.float32)
        update_direction_entry = expected / totals[:, None] - positive_keys
        return (update_direction_entry, jnp.log(totals) - positive_scores)
    directions, losses = lax.map(one_block, jnp.arange(block_count, dtype=jnp.int32))
    update_direction_entry = directions.reshape(NQ, D)
    loss_values = losses.reshape(NQ)
    question_derivative = update_direction_entry * (loss_multiplier / logit_divisor)[:, None]
    projection = lax.optimization_barrier(jnp.sum(query_floats * question_derivative, axis=1, keepdims=True))
    query_grad = query_scale * question_derivative - query_scale * query_scale * query_scale * query_floats * projection
    return (query_grad, loss_values)
```

```python
import functools

import jax
import jax.numpy as jnp
from jax import lax
from jax.experimental import pallas as pl
from jax.experimental.pallas import tpu as pltpu
from jax.sharding import PartitionSpec as P

logit_divisor = 0.1
epsilon = 1e-06
AXES = ("dp", "index")
LANES = 128
TAG_ROWS = 16
VMEM = pl.BlockSpec(memory_space=pltpu.VMEM)


def exchange(value, counts, flip):
    total = counts[0] * counts[1]
    return lax.ppermute(value, AXES, [(i, flip(i)) for i in range(total)])


def pack_kernel(keys_ref, clusters_ref, wire_ref):
    rows, width = keys_ref.shape
    floats = keys_ref[...].astype(jnp.float32)
    scale = lax.rsqrt(jnp.sum(floats * floats, axis=1, keepdims=True) + epsilon)
    unit = (floats * scale).astype(jnp.bfloat16)
    tiles = width // LANES
    for t in range(tiles):
        wire_ref[t * rows : (t + 1) * rows, :] = unit[:, t * LANES : (t + 1) * LANES]
    device = lax.axis_index("dp") * lax.axis_size("index") + lax.axis_index("index")
    place = lax.broadcasted_iota(jnp.int32, (TAG_ROWS, LANES), 1) % rows
    line = lax.broadcasted_iota(jnp.int32, (TAG_ROWS, LANES), 0)
    key_id = device * rows + place
    clusters = clusters_ref[...].reshape(1, rows)
    clusters = jnp.concatenate([clusters] * (LANES // rows), axis=1)
    tag = jnp.where(line == 0, clusters, jnp.where(line == 1, key_id // 256, key_id % 256))
    wire_ref[tiles * rows :, :] = tag.astype(jnp.float32).astype(jnp.bfloat16)


def pack(keys, clusters):
    rows, width = keys.shape
    return pl.pallas_call(
        pack_kernel,
        out_shape=jax.ShapeDtypeStruct((width // LANES * rows + TAG_ROWS, LANES), jnp.bfloat16),
        in_specs=[VMEM, VMEM],
        out_specs=VMEM,
        name="pack",
    )(keys, clusters)


def main_kernel(rows, group, queries_ref, pattern_ref, positives_ref, multiplier_ref, *refs):
    wires, (grad_ref, loss_ref, key_ref) = refs[:-3], refs[-3:]
    count, width = queries_ref.shape
    tiles = width // LANES
    per = LANES // rows
    wire_rows = tiles * rows + TAG_ROWS
    shards = [(wire, n * wire_rows) for wire in wires for n in range(wire.shape[0] // wire_rows)]
    lane = lax.broadcasted_iota(jnp.int32, (1, LANES), 1)
    diagonal = lax.broadcasted_iota(jnp.int32, (count, count), 0) == lax.broadcasted_iota(
        jnp.int32, (count, count), 1
    )

    def as_column(row):
        return jnp.sum(jnp.where(diagonal, row, 0.0), axis=1, keepdims=True)

    floats = queries_ref[...].astype(jnp.float32)
    scale = lax.rsqrt(jnp.sum(floats * floats, axis=1, keepdims=True) + epsilon)
    unit = (floats * scale).astype(jnp.bfloat16)
    positive = as_column(positives_ref[...].reshape(1, count).astype(jnp.float32))
    multiplier = as_column(multiplier_ref[...].reshape(1, count))
    clusters_all = pattern_ref.shape[1]
    marks = jnp.broadcast_to(
        pattern_ref[...].astype(jnp.float32).astype(jnp.bfloat16), (16, clusters_all)
    )

    def absorb(some):
        cluster_parts, id_parts = [], []
        for first in range(0, len(some), per):
            tag = None
            for j in range(per):
                wire, base = some[first + j]
                slot = (first + j) * rows
                for t in range(tiles):
                    key_ref[slot : slot + rows, t * LANES : (t + 1) * LANES] = wire[
                        base + t * rows : base + (t + 1) * rows, :
                    ]
                mine = wire[base + tiles * rows : base + wire_rows, :].astype(jnp.float32)
                tag = mine if tag is None else jnp.where(lane >= j * rows, mine, tag)
            cluster_parts.append(tag[0:1, :])
            id_parts.append(tag[1:2, :] * 256.0 + tag[2:3, :])
        cluster_row = jnp.concatenate(cluster_parts, axis=1)
        id_row = jnp.concatenate(id_parts, axis=1)
        keys = key_ref[: len(some) * rows, :]
        scores = (
            lax.dot_general(unit, keys, (((1,), (1,)), ((), ())), preferred_element_type=jnp.float32)
            / logit_divisor
        )
        onehot = (
            lax.broadcasted_iota(jnp.int32, (clusters_all, 1), 0).astype(jnp.float32) == cluster_row
        )
        allowed = lax.dot_general(
            marks,
            onehot.astype(jnp.float32).astype(jnp.bfloat16),
            (((1,), (0,)), ((), ())),
            preferred_element_type=jnp.float32,
        )[0:1, :]
        is_positive = (positive == id_row).astype(jnp.float32)
        weights = jnp.exp(scores) * jnp.maximum(allowed, is_positive)
        both = jnp.concatenate(
            [weights.astype(jnp.bfloat16), is_positive.astype(jnp.bfloat16)], axis=0
        )
        return (
            jnp.sum(weights, axis=1, keepdims=True),
            jnp.sum(scores * is_positive, axis=1, keepdims=True),
            lax.dot_general(both, keys, (((1,), (0,)), ((), ())), preferred_element_type=jnp.float32),
        )

    parts = [absorb(shards[first : first + group]) for first in range(0, len(shards), group)]
    totals, positive_score, sums = (functools.reduce(jnp.add, column) for column in zip(*parts))
    direction = sums[:count] / totals - sums[count:]
    gradient = direction * (multiplier / logit_divisor)
    projection = jnp.sum(floats * gradient, axis=1, keepdims=True)
    grad_ref[...] = scale * gradient - scale * scale * scale * floats * projection
    loss = jnp.log(totals) - positive_score
    loss_ref[...] = jnp.sum(jnp.where(diagonal, loss, 0.0), axis=0, keepdims=True).reshape(count)


def finish(rows, queries, pattern, positives, multiplier, wires):
    count, width = queries.shape
    wire_rows = width // LANES * rows + TAG_ROWS
    group = min(32, sum(wire.shape[0] // wire_rows for wire in wires))
    return pl.pallas_call(
        functools.partial(main_kernel, rows, group),
        out_shape=(
            jax.ShapeDtypeStruct((count, width), jnp.float32),
            jax.ShapeDtypeStruct((count,), jnp.float32),
        ),
        in_specs=[VMEM] * (4 + len(wires)),
        out_specs=(VMEM, VMEM),
        scratch_shapes=[pltpu.VMEM((group * rows, width), jnp.bfloat16)],
        compiler_params=pltpu.CompilerParams(vmem_limit_bytes=56 * 1024 * 1024),
        name="finish",
    )(queries, pattern, positives, multiplier, *wires)


def body(counts, queries, keys, pattern, clusters, positives, loss_multiplier):
    dp, index = counts
    rows = keys.shape[0]
    index_bits = index.bit_length() - 1
    dp_bits = dp.bit_length() - 1
    core = index_bits
    plane = list(range(index_bits + 1, index_bits + dp_bits))

    def along(value, bit):
        return exchange(value, counts, lambda i: i ^ (1 << bit))

    def along_plane(value, step):
        first, second = plane[step], plane[len(plane) - 1 - step]
        return exchange(
            value, counts, lambda i: i ^ (1 << (second if (i >> core) & 1 else first))
        )

    column = [pack(keys, clusters)]
    for bit in reversed(range(index_bits)):
        column += [along(value, bit) for value in column]
    if len(column) > 4:
        column = [jnp.concatenate(column, axis=0)]
    held = []
    for value in column:
        block = [value]
        for step in range(len(plane)):
            block += [along_plane(item, step) for item in block]
        held += block + [along(item, core) for item in block]
    return finish(rows, queries, pattern, positives, loss_multiplier, held)


def solution(mesh):
    counts = (mesh.shape["dp"], mesh.shape["index"])
    in_specs = (
        P(AXES, None),
        P(AXES, None),
        P(AXES, None),
        P(AXES),
        P(AXES),
        P(AXES),
    )
    out_specs = (P(AXES, None), P(AXES))
    return jax.shard_map(
        functools.partial(body, counts),
        mesh=mesh,
        in_specs=in_specs,
        out_specs=out_specs,
        check_vma=False,
    )
```

```python
import functools

import jax
import jax.numpy as jnp
from jax import lax
from jax.experimental import pallas as pl
from jax.experimental.pallas import tpu as pltpu
from jax.sharding import PartitionSpec as P

logit_divisor = 0.1
epsilon = 1e-06
AXES = ("dp", "index")
LANES = 128
TAG_ROWS = 16
VMEM = pl.BlockSpec(memory_space=pltpu.VMEM)


def exchange(value, counts, flip):
    total = counts[0] * counts[1]
    return lax.ppermute(value, AXES, [(i, flip(i)) for i in range(total)])


def pack_kernel(keys_ref, clusters_ref, wire_ref):
    rows, width = keys_ref.shape
    floats = keys_ref[...].astype(jnp.float32)
    scale = lax.rsqrt(jnp.sum(floats * floats, axis=1, keepdims=True) + epsilon)
    unit = (floats * scale).astype(jnp.bfloat16)
    tiles = width // LANES
    for t in range(tiles):
        wire_ref[t * rows : (t + 1) * rows, :] = unit[:, t * LANES : (t + 1) * LANES]
    device = lax.axis_index("dp") * lax.axis_size("index") + lax.axis_index("index")
    place = lax.broadcasted_iota(jnp.int32, (TAG_ROWS, LANES), 1) % rows
    line = lax.broadcasted_iota(jnp.int32, (TAG_ROWS, LANES), 0)
    key_id = device * rows + place
    clusters = clusters_ref[...].reshape(1, rows)
    clusters = jnp.concatenate([clusters] * (LANES // rows), axis=1)
    tag = jnp.where(line == 0, clusters, jnp.where(line == 1, key_id // 256, key_id % 256))
    wire_ref[tiles * rows :, :] = tag.astype(jnp.float32).astype(jnp.bfloat16)


def pack(keys, clusters):
    rows, width = keys.shape
    return pl.pallas_call(
        pack_kernel,
        out_shape=pltpu.VMEM((width // LANES * rows + TAG_ROWS, LANES), jnp.bfloat16),
        in_specs=[VMEM, VMEM],
        out_specs=VMEM,
        name="pack",
    )(keys, clusters)


def sum_kernel(rows, group, closing, priors, queries_ref, pattern_ref, positives_ref, *refs):
    refs = list(refs)
    multiplier_ref = refs.pop(0) if closing else None
    prior_refs = [(refs.pop(0), refs.pop(0)) for _ in range(priors)]
    key_ref, out_b, out_a = refs.pop(), refs.pop(), refs.pop()
    wires = refs
    count, width = queries_ref.shape
    tiles = width // LANES
    per = LANES // rows
    wire_rows = tiles * rows + TAG_ROWS
    shards = [(wire, n * wire_rows) for wire in wires for n in range(wire.shape[0] // wire_rows)]
    lane = lax.broadcasted_iota(jnp.int32, (1, LANES), 1)
    diagonal = lax.broadcasted_iota(jnp.int32, (count, count), 0) == lax.broadcasted_iota(
        jnp.int32, (count, count), 1
    )

    def as_column(row):
        return jnp.sum(jnp.where(diagonal, row, 0.0), axis=1, keepdims=True)

    floats = queries_ref[...].astype(jnp.float32)
    scale = lax.rsqrt(jnp.sum(floats * floats, axis=1, keepdims=True) + epsilon)
    unit = (floats * scale).astype(jnp.bfloat16)
    positive = as_column(positives_ref[...].reshape(1, count).astype(jnp.float32))
    clusters_all = pattern_ref.shape[1]
    marks = jnp.broadcast_to(
        pattern_ref[...].astype(jnp.float32).astype(jnp.bfloat16), (16, clusters_all)
    )

    def absorb(some):
        cluster_parts, id_parts = [], []
        for first in range(0, len(some), per):
            tag = None
            for j in range(per):
                wire, base = some[first + j]
                slot = (first + j) * rows
                for t in range(tiles):
                    key_ref[slot : slot + rows, t * LANES : (t + 1) * LANES] = wire[
                        base + t * rows : base + (t + 1) * rows, :
                    ]
                mine = wire[base + tiles * rows : base + wire_rows, :].astype(jnp.float32)
                tag = mine if tag is None else jnp.where(lane >= j * rows, mine, tag)
            cluster_parts.append(tag[0:1, :])
            id_parts.append(tag[1:2, :] * 256.0 + tag[2:3, :])
        cluster_row = jnp.concatenate(cluster_parts, axis=1)
        id_row = jnp.concatenate(id_parts, axis=1)
        keys = key_ref[: len(some) * rows, :]
        scores = (
            lax.dot_general(unit, keys, (((1,), (1,)), ((), ())), preferred_element_type=jnp.float32)
            / logit_divisor
        )
        onehot = (
            lax.broadcasted_iota(jnp.int32, (clusters_all, 1), 0).astype(jnp.float32) == cluster_row
        )
        allowed = lax.dot_general(
            marks,
            onehot.astype(jnp.float32).astype(jnp.bfloat16),
            (((1,), (0,)), ((), ())),
            preferred_element_type=jnp.float32,
        )[0:1, :]
        is_positive = (positive == id_row).astype(jnp.float32)
        weights = jnp.exp(scores) * jnp.maximum(allowed, is_positive)
        both = jnp.concatenate(
            [weights.astype(jnp.bfloat16), is_positive.astype(jnp.bfloat16)], axis=0
        )
        return (
            jnp.sum(weights, axis=1, keepdims=True),
            jnp.sum(scores * is_positive, axis=1, keepdims=True),
            lax.dot_general(both, keys, (((1,), (0,)), ((), ())), preferred_element_type=jnp.float32),
        )

    parts = [absorb(shards[first : first + group]) for first in range(0, len(shards), group)]
    for stats_ref, sums_ref in prior_refs:
        parts.append((stats_ref[:, 0:1], stats_ref[:, 1:2], sums_ref[...]))
    totals, positive_score, sums = (functools.reduce(jnp.add, column) for column in zip(*parts))
    if not closing:
        out_a[...] = jnp.where(lane == 0, totals, jnp.where(lane == 1, positive_score, 0.0))
        out_b[...] = sums
        return
    multiplier = as_column(multiplier_ref[...].reshape(1, count))
    direction = sums[:count] / totals - sums[count:]
    gradient = direction * (multiplier / logit_divisor)
    projection = jnp.sum(floats * gradient, axis=1, keepdims=True)
    out_a[...] = scale * gradient - scale * scale * scale * floats * projection
    loss = jnp.log(totals) - positive_score
    out_b[...] = jnp.sum(jnp.where(diagonal, loss, 0.0), axis=0, keepdims=True).reshape(count)


def sum_spans(rows, queries, pattern, positives, wires, multiplier=None, priors=(), cost=None):
    count, width = queries.shape
    wire_rows = width // LANES * rows + TAG_ROWS
    group = min(32, sum(wire.shape[0] // wire_rows for wire in wires))
    closing = multiplier is not None
    if closing:
        shapes = ((count, width), (count,))
    else:
        shapes = ((count, LANES), (2 * count, width))
    operands = [queries, pattern, positives] + [multiplier] * closing
    operands += [part for prior in priors for part in prior] + list(wires)
    return pl.pallas_call(
        functools.partial(sum_kernel, rows, group, closing, len(priors)),
        out_shape=tuple(jax.ShapeDtypeStruct(shape, jnp.float32) for shape in shapes),
        in_specs=[VMEM] * len(operands),
        out_specs=(VMEM, VMEM),
        scratch_shapes=[pltpu.VMEM((group * rows, width), jnp.bfloat16)],
        compiler_params=pltpu.CompilerParams(vmem_limit_bytes=24 * 1024 * 1024),
        cost_estimate=cost and pl.CostEstimate(flops=cost, bytes_accessed=0, transcendentals=0),
        name="close" if closing else "sum_spans",
    )(*operands)


def body(counts, queries, keys, pattern, clusters, positives, loss_multiplier):
    dp, index = counts
    rows = keys.shape[0]
    core = index.bit_length() - 1
    plane = list(range(core + 1, core + dp.bit_length() - 1))
    far = list(range(1, core))

    def along(value, bit):
        return exchange(value, counts, lambda i: i ^ (1 << bit))

    def join(values):
        return values[0] if len(values) == 1 else jnp.concatenate(values, axis=0)

    def both(values):
        value = join(values)
        return [value, along(value, core)]

    own = pack(keys, clusters)
    unit = own.shape[0]
    args = (rows, queries, pattern, positives)
    if len(plane) != 2 or len(far) != 1:
        return doubling(counts, args, own, loss_multiplier)

    bits = {1: plane[0], 2: plane[1], 4: 0, 8: far[0]}

    def go(value, *ways):
        flips = [sum(1 << place for bit, place in bits.items() if way & bit) for way in ways]
        return exchange(value, counts, lambda i: i ^ flips[(i >> core) & 1])

    def after(value, *earlier):
        return lax.optimization_barrier((value, *earlier))[0]

    v0 = own
    v1 = go(v0, 1, 2)
    v2_3 = go(join([v0, v1]), 2, 1)
    v4 = go(v0, 4, 4)
    v5 = go(v4, 1, 2)
    v6_7 = go(join([v4, v5]), 2, 1)
    v8 = go(v0, 8, 8)
    v9 = go(after(v8, v4), 1, 2)
    v10 = go(v8, 2, 1)
    v12 = go(v8, 4, 4)
    v14_11 = go(after(join([v12, v9]), v2_3), 2, 1)
    v13 = go(v9, 4, 4)
    v15 = go(after(v10, v10), 5, 6)
    part = sum_spans(*args, both([v0, v2_3, v4, v8, v9, v10]), cost=int(10000000000.0))
    return sum_spans(*args, both([v6_7, v14_11]) + both([v1, v5, v12, v13]) + both([v15]), loss_multiplier, [part])


def doubling(counts, args, own, loss_multiplier):
    dp, index = counts
    held = [own]
    for bit in range((dp * index).bit_length() - 1):
        if bit < index.bit_length() - 1:
            value = jnp.concatenate(held, axis=0) if len(held) > 1 else held[0]
            held = [value, exchange(value, counts, lambda i: i ^ (1 << bit))]
        else:
            if len(held) == 2 and bit == index.bit_length() - 1:
                held = [jnp.concatenate(held, axis=0)]
            held = held + [exchange(value, counts, lambda i: i ^ (1 << bit)) for value in held]
    parts = [sum_spans(*args, held[n : n + 4]) for n in range(4, len(held), 4)]
    return sum_spans(*args, held[:4], loss_multiplier, parts)


def solution(mesh):
    counts = (mesh.shape["dp"], mesh.shape["index"])
    in_specs = (
        P(AXES, None),
        P(AXES, None),
        P(AXES, None),
        P(AXES),
        P(AXES),
        P(AXES),
    )
    out_specs = (P(AXES, None), P(AXES))
    return jax.shard_map(
        functools.partial(body, counts),
        mesh=mesh,
        in_specs=in_specs,
        out_specs=out_specs,
        check_vma=False,
    )
```

```python
import functools

import jax
import jax.numpy as jnp
from jax import lax
from jax.experimental import pallas as pl
from jax.experimental.pallas import tpu as pltpu
from jax.sharding import PartitionSpec as P

logit_divisor = 0.1
epsilon = 1e-06
AXES = ("dp", "index")
LANES = 128
TAG_ROWS = 16
VMEM = pl.BlockSpec(memory_space=pltpu.VMEM)


def exchange(value, counts, flip):
    total = counts[0] * counts[1]
    return lax.ppermute(value, AXES, [(i, flip(i)) for i in range(total)])


def pack_kernel(keys_ref, clusters_ref, wire_ref):
    rows, width = keys_ref.shape
    floats = keys_ref[...].astype(jnp.float32)
    scale = lax.rsqrt(jnp.sum(floats * floats, axis=1, keepdims=True) + epsilon)
    unit = (floats * scale).astype(jnp.bfloat16)
    tiles = width // LANES
    for t in range(tiles):
        wire_ref[t * rows : (t + 1) * rows, :] = unit[:, t * LANES : (t + 1) * LANES]
    device = lax.axis_index("dp") * lax.axis_size("index") + lax.axis_index("index")
    place = lax.broadcasted_iota(jnp.int32, (TAG_ROWS, LANES), 1) % rows
    line = lax.broadcasted_iota(jnp.int32, (TAG_ROWS, LANES), 0)
    key_id = device * rows + place
    clusters = clusters_ref[...].reshape(1, rows)
    clusters = jnp.concatenate([clusters] * (LANES // rows), axis=1)
    tag = jnp.where(line == 0, clusters, jnp.where(line == 1, key_id // 256, key_id % 256))
    wire_ref[tiles * rows :, :] = tag.astype(jnp.float32).astype(jnp.bfloat16)


def pack(keys, clusters):
    rows, width = keys.shape
    return pl.pallas_call(
        pack_kernel,
        out_shape=pltpu.VMEM((width // LANES * rows + TAG_ROWS, LANES), jnp.bfloat16),
        in_specs=[VMEM, VMEM],
        out_specs=VMEM,
        name="pack",
    )(keys, clusters)


def sum_kernel(rows, group, closing, priors, queries_ref, pattern_ref, positives_ref, *refs):
    refs = list(refs)
    multiplier_ref = refs.pop(0) if closing else None
    prior_refs = [(refs.pop(0), refs.pop(0)) for _ in range(priors)]
    key_ref, out_b, out_a = refs.pop(), refs.pop(), refs.pop()
    wires = refs
    count, width = queries_ref.shape
    tiles = width // LANES
    per = LANES // rows
    wire_rows = tiles * rows + TAG_ROWS
    shards = [(wire, n * wire_rows) for wire in wires for n in range(wire.shape[0] // wire_rows)]
    lane = lax.broadcasted_iota(jnp.int32, (1, LANES), 1)
    diagonal = lax.broadcasted_iota(jnp.int32, (count, count), 0) == lax.broadcasted_iota(
        jnp.int32, (count, count), 1
    )

    def as_column(row):
        return jnp.sum(jnp.where(diagonal, row, 0.0), axis=1, keepdims=True)

    floats = queries_ref[...].astype(jnp.float32)
    scale = lax.rsqrt(jnp.sum(floats * floats, axis=1, keepdims=True) + epsilon)
    unit = (floats * scale).astype(jnp.bfloat16)
    positive = as_column(positives_ref[...].reshape(1, count).astype(jnp.float32))
    clusters_all = pattern_ref.shape[1]
    marks = jnp.broadcast_to(
        pattern_ref[...].astype(jnp.float32).astype(jnp.bfloat16), (16, clusters_all)
    )

    def absorb(some):
        cluster_parts, id_parts = [], []
        for first in range(0, len(some), per):
            tag = None
            for j in range(per):
                wire, base = some[first + j]
                slot = (first + j) * rows
                for t in range(tiles):
                    key_ref[slot : slot + rows, t * LANES : (t + 1) * LANES] = wire[
                        base + t * rows : base + (t + 1) * rows, :
                    ]
                mine = wire[base + tiles * rows : base + wire_rows, :].astype(jnp.float32)
                tag = mine if tag is None else jnp.where(lane >= j * rows, mine, tag)
            cluster_parts.append(tag[0:1, :])
            id_parts.append(tag[1:2, :] * 256.0 + tag[2:3, :])
        cluster_row = jnp.concatenate(cluster_parts, axis=1)
        id_row = jnp.concatenate(id_parts, axis=1)
        keys = key_ref[: len(some) * rows, :]
        scores = (
            lax.dot_general(unit, keys, (((1,), (1,)), ((), ())), preferred_element_type=jnp.float32)
            / logit_divisor
        )
        onehot = (
            lax.broadcasted_iota(jnp.int32, (clusters_all, 1), 0).astype(jnp.float32) == cluster_row
        )
        allowed = lax.dot_general(
            marks,
            onehot.astype(jnp.float32).astype(jnp.bfloat16),
            (((1,), (0,)), ((), ())),
            preferred_element_type=jnp.float32,
        )[0:1, :]
        is_positive = (positive == id_row).astype(jnp.float32)
        weights = jnp.exp(scores) * jnp.maximum(allowed, is_positive)
        both = jnp.concatenate(
            [weights.astype(jnp.bfloat16), is_positive.astype(jnp.bfloat16)], axis=0
        )
        return (
            jnp.sum(weights, axis=1, keepdims=True),
            jnp.sum(scores * is_positive, axis=1, keepdims=True),
            lax.dot_general(both, keys, (((1,), (0,)), ((), ())), preferred_element_type=jnp.float32),
        )

    parts = [absorb(shards[first : first + group]) for first in range(0, len(shards), group)]
    for stats_ref, sums_ref in prior_refs:
        parts.append((stats_ref[:, 0:1], stats_ref[:, 1:2], sums_ref[...]))
    totals, positive_score, sums = (functools.reduce(jnp.add, column) for column in zip(*parts))
    if not closing:
        out_a[...] = jnp.where(lane == 0, totals, jnp.where(lane == 1, positive_score, 0.0))
        out_b[...] = sums
        return
    multiplier = as_column(multiplier_ref[...].reshape(1, count))
    direction = sums[:count] / totals - sums[count:]
    gradient = direction * (multiplier / logit_divisor)
    projection = jnp.sum(floats * gradient, axis=1, keepdims=True)
    out_a[...] = scale * gradient - scale * scale * scale * floats * projection
    loss = jnp.log(totals) - positive_score
    out_b[...] = jnp.sum(jnp.where(diagonal, loss, 0.0), axis=0, keepdims=True).reshape(count)


def sum_spans(rows, queries, pattern, positives, wires, multiplier=None, priors=(), cost=None):
    count, width = queries.shape
    wire_rows = width // LANES * rows + TAG_ROWS
    group = min(32, sum(wire.shape[0] // wire_rows for wire in wires))
    closing = multiplier is not None
    if closing:
        shapes = ((count, width), (count,))
    else:
        shapes = ((count, LANES), (2 * count, width))
    operands = [queries, pattern, positives] + [multiplier] * closing
    operands += [part for prior in priors for part in prior] + list(wires)
    return pl.pallas_call(
        functools.partial(sum_kernel, rows, group, closing, len(priors)),
        out_shape=tuple(jax.ShapeDtypeStruct(shape, jnp.float32) for shape in shapes),
        in_specs=[VMEM] * len(operands),
        out_specs=(VMEM, VMEM),
        scratch_shapes=[pltpu.VMEM((group * rows, width), jnp.bfloat16)],
        compiler_params=pltpu.CompilerParams(vmem_limit_bytes=24 * 1024 * 1024),
        cost_estimate=cost and pl.CostEstimate(flops=cost, bytes_accessed=0, transcendentals=0),
        name="close" if closing else "sum_spans",
    )(*operands)


def body(counts, queries, keys, pattern, clusters, positives, loss_multiplier):
    dp, index = counts
    rows = keys.shape[0]
    core = index.bit_length() - 1
    plane = list(range(core + 1, core + dp.bit_length() - 1))
    far = list(range(1, core))

    def along(value, bit):
        return exchange(value, counts, lambda i: i ^ (1 << bit))

    def join(values):
        return values[0] if len(values) == 1 else jnp.concatenate(values, axis=0)

    def after(value, *earlier):
        return lax.optimization_barrier((value, *earlier))[0] if earlier else value

    def both(values, *earlier):
        value = join(values)
        return [value, along(after(value, *earlier), core)]

    own = pack(keys, clusters)
    unit = own.shape[0]
    args = (rows, queries, pattern, positives)
    if len(plane) != 2 or len(far) != 1:
        return doubling(counts, args, own, loss_multiplier)

    bits = {1: plane[0], 2: plane[1], 4: 0, 8: far[0]}

    def go(value, *ways):
        flips = [sum(1 << place for bit, place in bits.items() if way & bit) for way in ways]
        return exchange(value, counts, lambda i: i ^ flips[(i >> core) & 1])

    v0 = own
    v1 = go(v0, 1, 2)
    v2_3 = go(join([v0, v1]), 2, 4)
    v4 = go(v0, 4, 1)
    v5 = go(v4, 1, 2)
    v6_7 = go(join([v4, v5]), 2, 4)
    v8 = go(v0, 8, 8)
    v9 = go(after(v8, v4), 1, 2)
    v10 = go(v8, 2, 4)
    v12 = go(v8, 4, 1)
    v14_11 = go(after(join([v12, v9]), v2_3), 2, 4)
    v13 = go(after(v9, v4), 4, 1)
    v15 = go(v10, 5, 3)
    part = sum_spans(*args, both([v0, v1, v2_3, v4, v5, v8, v9]) + both([v6_7[0*unit:1*unit], v10, v12]), cost=int(4000000000.0))
    return sum_spans(*args, both([v6_7[1*unit:2*unit], v14_11, v13, v15]), loss_multiplier, [part])


def doubling(counts, args, own, loss_multiplier):
    dp, index = counts
    held = [own]
    for bit in range((dp * index).bit_length() - 1):
        if bit < index.bit_length() - 1:
            value = jnp.concatenate(held, axis=0) if len(held) > 1 else held[0]
            held = [value, exchange(value, counts, lambda i: i ^ (1 << bit))]
        else:
            if len(held) == 2 and bit == index.bit_length() - 1:
                held = [jnp.concatenate(held, axis=0)]
            held = held + [exchange(value, counts, lambda i: i ^ (1 << bit)) for value in held]
    parts = [sum_spans(*args, held[n : n + 4]) for n in range(4, len(held), 4)]
    return sum_spans(*args, held[:4], loss_multiplier, parts)


def solution(mesh):
    counts = (mesh.shape["dp"], mesh.shape["index"])
    in_specs = (
        P(AXES, None),
        P(AXES, None),
        P(AXES, None),
        P(AXES),
        P(AXES),
        P(AXES),
    )
    out_specs = (P(AXES, None), P(AXES))
    return jax.shard_map(
        functools.partial(body, counts),
        mesh=mesh,
        in_specs=in_specs,
        out_specs=out_specs,
        check_vma=False,
    )
```
